32 devices in a mesh: band: 4 (over y, x), dom: 8 (over z, core).
Axes of the slice: x: 2, y: 2, z: 4, core: 2. Of those that a mesh axis runs over, the one named last changes fastest.
Arguments:
- orbitals: float32 [16, 32, 32, 1024], P('dom', None, None, 'band'), may hold values from -6 to 6
- potential: float32 [16, 32, 32], P('dom'), may hold values from -2 to 2
- projectors: float32 [1024, 8, 256], P('dom'), may hold values from -0.375 to 0.375
- tile_cells: int32 [1024, 256], P('dom'), may hold values from 0 to 2047
- tile_atom: int32 [1024], replicated, may hold values from -1 to 63, as said below
- atom_owner: int32 [64], replicated, may hold values from 0 to 63, as said below
- coupling: float32 [64, 8, 8], P('dom'), may hold values from -2 to 2
- rotation: float32 [1024, 1024], P(None, 'band'), may hold values from -0.1875 to 0.1875
Outputs:
- rotated_orbitals: float32 [16, 32, 32, 1024], P('dom', None, None, 'band')
- rotated_applied: float32 [16, 32, 32, 1024], P('dom', None, None, 'band')
The draws below stay inside these ranges and needn't reach their ends.
Inputs may be any that keep to these rules, and one draw needn't show every extreme that they name: `tile_atom`: tile slots come in blocks of 128, one block a domain; in each block the used slots come first, at least half of them are used, and some block is full. An atom a is owned by domain atom_owner[a] // 8. The tiles of one domain name atoms of any one owning domain at most 32 times, and some owning domain is named exactly 32 times by every domain. `atom_owner`: each row of the coupling table belongs to exactly one atom.
All inputs are finite; a program needn't handle non-finite values.
Results may differ from the reference program's by a relative error of at most 0.000071.
Values sent between devices are 32-bit elements; how exact they have to be, the bound alone decides.
A program may use at most 128 MiB of HBM per device.

```python
import jax
import jax.numpy as jnp
from jax import lax

BANDS = 1024
NPROJ = 8
CX = 2
NY = 32
NZ = 32
TILE = 256
E_DEV = 128
ATOM_DEV = 8
NX = 16
NATOM = 64
ENTRIES = 1024
N_DOM = 8


def domain_order(pool_key):
    return jax.random.permutation(pool_key, N_DOM * max(2, 2 * E_DEV // N_DOM))


def atom_tables(key):
    atom_total = ATOM_DEV * N_DOM
    capacity = max(2, 2 * E_DEV // N_DOM)
    pool_size = N_DOM * capacity
    atom_rows = jax.random.permutation(jax.random.fold_in(key, 11), atom_total).astype(jnp.int32)
    row_atoms = jnp.argsort(atom_rows).astype(jnp.int32)
    busiest = jax.random.randint(jax.random.fold_in(key, 12), (), 0, N_DOM)
    fullest = jax.random.randint(jax.random.fold_in(key, 13), (), 0, N_DOM)
    counts = jax.random.randint(jax.random.fold_in(key, 14), (N_DOM,), E_DEV // 2, E_DEV + 1)
    counts = jnp.where(jnp.arange(N_DOM) == fullest, E_DEV, counts)
    owner_pool = jnp.arange(pool_size, dtype=jnp.int32) // capacity
    domain_keys = jax.random.split(jax.random.fold_in(key, 15), N_DOM)
    scores = jax.vmap(domain_order)(domain_keys).astype(jnp.int32)
    scores = jnp.where(owner_pool[None, :] == busiest, scores - pool_size, scores)
    picked = jnp.argsort(scores, axis=1)[:, :E_DEV]
    owners = owner_pool[picked]
    slot_draw = jax.random.randint(jax.random.fold_in(key, 16), (N_DOM, E_DEV), 0, ATOM_DEV)
    atom_ids = row_atoms[owners * ATOM_DEV + slot_draw]
    used_mask = jnp.arange(E_DEV)[None, :] < counts[:, None]
    tile_list = jnp.where(used_mask, atom_ids, -1).reshape(-1).astype(jnp.int32)
    return (atom_rows, tile_list)


def draw_tile_atom(key, part):
    return atom_tables(key)[1]


def draw_atom_owner(key, part):
    return atom_tables(key)[0]


def touch_ends(array, key, low, high):
    dims = array.shape
    spot = [jax.random.randint(jax.random.fold_in(key, axis), (), 0, dims[axis]) for axis in range(len(dims))]
    array = array.at[tuple(spot)].set(low)
    longest = dims.index(max(dims))
    spot[longest] = (spot[longest] + 1) % dims[longest]
    return array.at[tuple(spot)].set(high)


def block_scale(rng, shape, cuts, smallest, top_value):
    factor_of = 1.0
    for axis_at, blocks in cuts:
        draws = jax.random.uniform(jax.random.fold_in(jax.random.fold_in(rng, 6), axis_at), (blocks,), jnp.float32, smallest / len(cuts), top_value / len(cuts))
        factor_of = factor_of * jnp.repeat(jnp.exp(draws), shape[axis_at] // blocks).reshape((-1,) + (1,) * (len(shape) - 1 - axis_at))
    return factor_of


def normal_values(key, shape, scale, bound, shards=(), kind=jnp.bfloat16):
    values = jax.random.normal(key, shape, jnp.float32) * scale
    if len(shards) > 0:
        values = block_scale(key, shape, shards, -0.22, 0.18) * values
    return jnp.clip(values, min=-bound, max=bound).astype(kind)


def setup_inputs(seed: int = 0) -> dict:
    key_list = jax.random.split(jax.random.key(seed), 9)
    return {
        "orbitals": normal_values(key_list[0], (NX, NY, NZ, BANDS), 1.0, 6.0, ((0, 8), (3, 4)), jnp.float32),
        "potential": jnp.clip(jax.random.uniform(key_list[1], (NX, NY, NZ), jnp.float32, -2.0, 2.0) * block_scale(key_list[1], (NX, NY, NZ), ((0, 8),), -0.4, 0.0), -2.0, 2.0),
        "projectors": normal_values(key_list[2], (ENTRIES, NPROJ, TILE), TILE ** -0.5, 0.375, ((0, 8),), jnp.float32),
        "tile_cells": touch_ends(jax.random.randint(key_list[3], (ENTRIES, TILE), 0, CX * NY * NZ), jax.random.fold_in(key_list[3], 1), 0, (CX * NY * NZ) - 1).astype(jnp.int32),
        "tile_atom": draw_tile_atom(jax.random.fold_in(key_list[8], 71), 0),
        "atom_owner": draw_atom_owner(jax.random.fold_in(key_list[8], 71), 0),
        "coupling": normal_values(key_list[6], (NATOM, NPROJ, NPROJ), NPROJ ** -0.5, 2.0, ((0, 8),), jnp.float32),
        "rotation": normal_values(key_list[7], (BANDS, BANDS), BANDS ** -0.5, 0.1875, ((1, 4),), jnp.float32),
    }


def neighbor_sum(field):
    summed = jnp.roll(field, 1, 0) + jnp.roll(field, -1, 0)
    summed = summed + jnp.roll(field, 1, 1) + jnp.roll(field, -1, 1)
    return summed + jnp.roll(field, 1, 2) + jnp.roll(field, -1, 2)


def reference(orbitals, potential, projectors, tile_cells, tile_atom, atom_owner, coupling, rotation):
    band_count = orbitals.shape[3]
    cell_count = CX * NY * NZ
    applied_local = (3.0 + potential[..., None]) * orbitals - 0.5 * neighbor_sum(orbitals)
    domain_fields = orbitals.reshape(N_DOM, cell_count, band_count)
    domain_cells = tile_cells.reshape(N_DOM, E_DEV, TILE)
    domain_projectors = projectors.reshape(N_DOM, E_DEV, NPROJ, TILE)

    def project(inputs):
        domain_field, tile_index, values = inputs
        gathered = jnp.take(domain_field, tile_index.reshape(-1), axis=0).reshape(E_DEV, TILE, band_count)
        return jnp.einsum("ekt,etb->ekb", values, gathered, precision=lax.Precision.HIGHEST)

    partials = lax.map(project, (domain_fields, domain_cells, domain_projectors)).reshape(ENTRIES, NPROJ, band_count)
    used_mask = tile_atom >= 0
    segment = jnp.where(used_mask, tile_atom, NATOM).astype(jnp.int32)
    atom_sums = jax.ops.segment_sum(partials, segment, num_segments=NATOM + 1)[:NATOM]
    atom_coupling = coupling[atom_owner]
    scaled = jnp.einsum("akj,ajb->akb", atom_coupling, atom_sums, precision=lax.Precision.HIGHEST)
    safe_atom = jnp.where(used_mask, tile_atom, 0).astype(jnp.int32)
    returned = jnp.take(scaled, safe_atom, axis=0) * used_mask[:, None, None].astype(jnp.float32)
    domain_returned = returned.reshape(N_DOM, E_DEV, NPROJ, band_count)

    def expand(inputs):
        tile_index, values, coefficient = inputs
        spread = jnp.einsum("ekt,ekb->etb", values, coefficient, precision=lax.Precision.HIGHEST)
        spread = spread.reshape(E_DEV * TILE, band_count)
        return jnp.zeros((cell_count, band_count), jnp.float32).at[tile_index.reshape(-1)].add(spread)

    applied_far = lax.map(expand, (domain_cells, domain_projectors, domain_returned)).reshape(orbitals.shape)
    applied = applied_local + applied_far
    rotated_orbitals = jnp.dot(orbitals.reshape(-1, band_count), rotation, precision=lax.Precision.HIGHEST, preferred_element_type=jnp.float32).reshape(orbitals.shape)
    rotated_applied = jnp.dot(applied.reshape(-1, band_count), rotation, precision=lax.Precision.HIGHEST, preferred_element_type=jnp.float32).reshape(orbitals.shape)
    return rotated_orbitals, rotated_applied
```

```python
import functools

import jax
import jax.numpy as jnp
from jax import lax
from jax.experimental import pallas as pl
from jax.experimental.pallas import tpu as pltpu
from jax.sharding import PartitionSpec as P

LANES = 128
SUB = 8


def split(x):
    high = x.astype(jnp.bfloat16)
    low = (x - high.astype(jnp.float32)).astype(jnp.bfloat16)
    return high, low


def split_outside(x):
    high = lax.reduce_precision(x, exponent_bits=8, mantissa_bits=7)
    return high.astype(jnp.bfloat16), (x - high).astype(jnp.bfloat16)


def dot3(a, b, dims=(((1,), (0,)), ((), ()))):
    a_high, a_low = a
    b_high, b_low = b
    dot = functools.partial(lax.dot_general, dimension_numbers=dims, preferred_element_type=jnp.float32)
    return dot(a_high, b_high) + (dot(a_high, b_low) + dot(a_low, b_high))


def owner_rows(atom_ids, atom_owner):
    match = atom_ids[..., None] == jnp.arange(atom_owner.shape[0], dtype=jnp.int32)
    found_rows = jnp.sum(jnp.where(match, atom_owner, 0), axis=-1)
    return jnp.where(atom_ids >= 0, found_rows, -1)


def project_kernel(cells_ref, values_ref, high_ref, low_ref, dense_high, dense_low, partials_ref):
    tiles, proj, tile = values_ref.shape
    groups = dense_high.shape[1] // LANES
    lane_ids = lax.broadcasted_iota(jnp.int32, (LANES, tile), 0)

    def step(e, carry):
        cells = cells_ref[pl.ds(e, 1), :]
        group = jnp.broadcast_to(cells // LANES, (proj, tile))
        spot = jnp.broadcast_to(cells % LANES, (LANES, tile))
        hot = jnp.where(spot == lane_ids, 1.0, 0.0).astype(jnp.bfloat16)
        values = values_ref[e]
        high = values.astype(jnp.bfloat16).astype(jnp.float32)
        low = values - high
        rows = [jnp.where(group == g, high, 0.0) for g in range(groups)]
        rows += [jnp.where(group == g, low, 0.0) for g in range(groups)]
        left = jnp.concatenate(rows, axis=0).astype(jnp.bfloat16)
        out = lax.dot_general(
            left, hot, (((1,), (1,)), ((), ())), preferred_element_type=jnp.float32
        )
        half = groups * proj
        total = out[:half] + out[half:]
        row = jnp.concatenate([total[g * proj : (g + 1) * proj] for g in range(groups)], axis=1)
        return row

    def pair(i, carry):
        both = jnp.concatenate([step(2 * i, None), step(2 * i + 1, None)], axis=0)
        high, low = split(both)
        at = pl.ds(pl.multiple_of(i * 2 * proj, 2 * proj), 2 * proj)
        dense_high[at, :] = high
        dense_low[at, :] = low
        return carry

    lax.fori_loop(0, tiles // 2, pair, 0)
    partials_ref[...] = dot3(
        (dense_high[...], dense_low[...]), (high_ref[...], low_ref[...])
    )


def project(tile_cells, projectors, field_high, field_low):
    entries, proj, tile = projectors.shape
    cell_count, bands = field_high.shape
    block = 16
    rows = block * proj
    flops = 2 * entries * (2 * proj * cell_count * tile + 3 * proj * cell_count * bands)
    return pl.pallas_call(
        project_kernel,
        grid=(entries // block,),
        in_specs=[
            pl.BlockSpec((block, tile), lambda i: (i, 0)),
            pl.BlockSpec((block, proj, tile), lambda i: (i, 0, 0)),
            pl.BlockSpec((cell_count, bands), lambda i: (0, 0)),
            pl.BlockSpec((cell_count, bands), lambda i: (0, 0)),
        ],
        out_specs=[
            pl.BlockSpec((rows, cell_count), lambda i: (i, 0)),
            pl.BlockSpec((rows, cell_count), lambda i: (i, 0)),
            pl.BlockSpec((rows, bands), lambda i: (i, 0)),
        ],
        out_shape=[
            jax.ShapeDtypeStruct((entries * proj, cell_count), jnp.bfloat16),
            jax.ShapeDtypeStruct((entries * proj, cell_count), jnp.bfloat16),
            jax.ShapeDtypeStruct((entries * proj, bands), jnp.float32),
        ],
        compiler_params=pltpu.CompilerParams(vmem_limit_bytes=32 * 2**20),
        cost_estimate=pl.CostEstimate(flops=8 * flops, bytes_accessed=2**24, transcendentals=0),
        name="project",
    )(tile_cells, projectors, field_high, field_low)


def spread_kernel(dense_high, dense_low, back_high, back_low, far_ref):
    dims = (((0,), (0,)), ((), ()))
    far_ref[...] = dot3(
        (dense_high[...], dense_low[...]), (back_high[...], back_low[...]), dims
    )


def spread(dense_high, dense_low, back):
    rows, cell_count = dense_high.shape
    bands = back.shape[1]
    block = 256
    back_high, back_low = split_outside(back)
    return pl.pallas_call(
        spread_kernel,
        grid=(cell_count // block,),
        in_specs=[
            pl.BlockSpec((rows, block), lambda i: (0, i)),
            pl.BlockSpec((rows, block), lambda i: (0, i)),
            pl.BlockSpec((rows, bands), lambda i: (0, 0)),
            pl.BlockSpec((rows, bands), lambda i: (0, 0)),
        ],
        out_specs=pl.BlockSpec((block, bands), lambda i: (i, 0)),
        out_shape=jax.ShapeDtypeStruct((cell_count, bands), jnp.float32),
        compiler_params=pltpu.CompilerParams(vmem_limit_bytes=32 * 2**20),
        cost_estimate=pl.CostEstimate(
            flops=6 * rows * cell_count * bands, bytes_accessed=2**24, transcendentals=0
        ),
        name="spread",
    )(dense_high, dense_low, back_high, back_low)


def rotate_kernel(count, *refs):
    blocks, mats, out_ref = refs[:count], refs[count:-1], refs[-1]
    total = None
    for block, mat in zip(blocks, mats):
        term = dot3(split(block[...]), split(mat[...]))
        total = term if total is None else total + term
    out_ref[...] = total


def rotate(blocks, mats):
    rows, depth = blocks[0].shape
    bands = mats[0].shape[1]
    block = 256
    return pl.pallas_call(
        functools.partial(rotate_kernel, len(blocks)),
        grid=(rows // block,),
        in_specs=[pl.BlockSpec((block, depth), lambda i: (i, 0))] * len(blocks)
        + [pl.BlockSpec((depth, bands), lambda i: (0, 0))] * len(mats),
        out_specs=pl.BlockSpec((block, bands), lambda i: (i, 0)),
        out_shape=jax.ShapeDtypeStruct((rows, bands), jnp.float32),
        compiler_params=pltpu.CompilerParams(vmem_limit_bytes=32 * 2**20),
        cost_estimate=pl.CostEstimate(
            flops=6 * rows * depth * len(blocks) * bands, bytes_accessed=2**22, transcendentals=0
        ),
        name="rotate",
    )(*blocks, *mats)


def local_kernel(field_ref, before_ref, after_ref, weight_ref, far_ref, out_ref):
    planes = field_ref.shape[0]
    for p in range(planes):
        here = field_ref[p]
        low = before_ref[...] if p == 0 else field_ref[p - 1]
        high = after_ref[...] if p == planes - 1 else field_ref[p + 1]
        beside = low + high
        beside = beside + jnp.roll(here, 1, 0) + jnp.roll(here, -1, 0)
        beside = beside + jnp.roll(here, 1, 1) + jnp.roll(here, -1, 1)
        out_ref[p] = weight_ref[p] * here - 0.5 * beside + far_ref[p]


def local_apply(field, before, after, weight, far):
    planes, ny, nz, bands = field.shape
    whole = pl.BlockSpec((planes, ny, nz, LANES), lambda i: (0, 0, 0, i))
    side = pl.BlockSpec((ny, nz, LANES), lambda i: (0, 0, i))
    return pl.pallas_call(
        local_kernel,
        grid=(bands // LANES,),
        in_specs=[
            whole,
            side,
            side,
            pl.BlockSpec((planes, ny, nz, LANES), lambda i: (0, 0, 0, 0)),
            whole,
        ],
        out_specs=whole,
        out_shape=jax.ShapeDtypeStruct(field.shape, jnp.float32),
        compiler_params=pltpu.CompilerParams(vmem_limit_bytes=40 * 2**20),
        cost_estimate=pl.CostEstimate(
            flops=12 * planes * ny * nz * bands, bytes_accessed=2**23, transcendentals=0
        ),
        name="local",
    )(field, before, after, weight, far)


def gather_blocks(field, parts):
    count = lax.axis_size("band")
    me = lax.axis_index("band")
    rows = field.shape[0] // parts
    pieces = [field[i * rows : (i + 1) * rows] for i in range(parts)]
    if count != 4:
        out = []
        for piece in pieces:
            whole = lax.all_gather(piece, "band", axis=0)
            out.append([whole[i] for i in range(count)])
        return out, list(range(count))
    flip = lambda k: [(i, i ^ k) for i in range(count)]
    out = []
    for piece in pieces:
        one = lax.ppermute(piece, "band", flip(1))
        two = lax.ppermute(piece, "band", flip(2))
        half = rows // 2
        three = jnp.concatenate(
            [
                lax.ppermute(one[:half], "band", flip(2)),
                lax.ppermute(two[half:], "band", flip(1)),
            ],
            axis=0,
        )
        out.append([piece, one, two, three])
    return out, [me ^ k for k in range(count)]


def body(orbitals, potential, projectors, tile_cells, tile_atom, atom_owner, coupling, rotation):
    planes, ny, nz, bands = orbitals.shape
    cell_count = planes * ny * nz
    entries, proj, _ = projectors.shape
    atom_total = atom_owner.shape[0]
    dom_count = lax.axis_size("dom")
    domain_index = lax.axis_index("dom")
    field = orbitals.reshape(cell_count, bands)
    blocks, owners = gather_blocks(field, planes)
    mats = [lax.dynamic_slice_in_dim(rotation, o * bands, bands, axis=0) for o in owners]

    field_high, field_low = split_outside(field)
    dense_high, dense_low, partials = project(tile_cells, projectors, field_high, field_low)
    my_atoms = lax.dynamic_slice_in_dim(tile_atom, domain_index * entries, entries)
    my_rows = owner_rows(my_atoms, atom_owner)
    columns = (my_rows[:, None] == jnp.arange(atom_total, dtype=jnp.int32)[None, :]).astype(
        jnp.float32
    )
    sums = jnp.einsum(
        "ea,ekb->akb",
        columns,
        partials.reshape(entries, proj, bands),
        precision=lax.Precision.HIGHEST,
    )
    owned = lax.psum_scatter(sums, "dom", scatter_dimension=0, tiled=True)
    scaled = jnp.einsum("akj,ajb->akb", coupling, owned, precision=lax.Precision.HIGHEST)
    scaled = scaled.reshape(-1, bands)
    scaled = lax.all_gather(scaled, "band", axis=1, tiled=True)
    scaled = jnp.dot(scaled, rotation, precision=lax.Precision.HIGHEST)
    scaled = lax.all_gather(scaled, "dom", axis=0, tiled=True).reshape(atom_total, proj, bands)
    back = jnp.einsum("ea,akb->ekb", columns, scaled, precision=lax.Precision.HIGHEST)
    far = spread(dense_high, dense_low, back.reshape(entries * proj, bands))

    weight = jnp.broadcast_to((3.0 + potential)[..., None], (planes, ny, nz, LANES))
    rotated = [rotate(part, mats).reshape(ny, nz, bands) for part in blocks]
    after = lax.ppermute(rotated[0], "dom", [((i + 1) % dom_count, i) for i in range(dom_count)])
    before = lax.ppermute(rotated[-1], "dom", [(i, (i + 1) % dom_count) for i in range(dom_count)])
    first = jnp.stack(rotated, axis=0)
    second = local_apply(first, before, after, weight, far.reshape(orbitals.shape))
    return first, second


def solution(mesh):
    return jax.shard_map(
        body,
        mesh=mesh,
        in_specs=(
            P("dom", None, None, "band"),
            P("dom", None, None),
            P("dom", None, None),
            P("dom", None),
            P(),
            P(),
            P("dom", None, None),
            P(None, "band"),
        ),
        out_specs=(P("dom", None, None, "band"), P("dom", None, None, "band")),
        check_vma=False,
    )
```

```python
import functools

import jax
import jax.numpy as jnp
from jax import lax
from jax.experimental import pallas as pl
from jax.experimental.pallas import tpu as pltpu
from jax.sharding import PartitionSpec as P

LANES = 128
SUB = 8


def split(x):
    high = x.astype(jnp.bfloat16)
    low = (x - high.astype(jnp.float32)).astype(jnp.bfloat16)
    return high, low


def split_outside(x):
    high = lax.reduce_precision(x, exponent_bits=8, mantissa_bits=7)
    return high.astype(jnp.bfloat16), (x - high).astype(jnp.bfloat16)


def dot3(a, b, dims=(((1,), (0,)), ((), ()))):
    a_high, a_low = a
    b_high, b_low = b
    dot = functools.partial(lax.dot_general, dimension_numbers=dims, preferred_element_type=jnp.float32)
    return dot(a_high, b_high) + (dot(a_high, b_low) + dot(a_low, b_high))


def owner_rows(atom_ids, atom_owner):
    match = atom_ids[..., None] == jnp.arange(atom_owner.shape[0], dtype=jnp.int32)
    found_rows = jnp.sum(jnp.where(match, atom_owner, 0), axis=-1)
    return jnp.where(atom_ids >= 0, found_rows, -1)


def project_kernel(
    cells_ref, values_ref, field_ref, dense_high, dense_low, partials_ref, high_ref, low_ref
):
    @pl.when(pl.program_id(0) == 0)
    def _():
        high_ref[...], low_ref[...] = split(field_ref[...])

    tiles, proj, tile = values_ref.shape
    groups = dense_high.shape[1] // LANES
    lane_ids = lax.broadcasted_iota(jnp.int32, (LANES, tile), 0)

    def step(e, carry):
        cells = cells_ref[pl.ds(e, 1), :]
        group = jnp.broadcast_to(cells // LANES, (proj, tile))
        spot = jnp.broadcast_to(cells % LANES, (LANES, tile))
        hot = jnp.where(spot == lane_ids, 1.0, 0.0).astype(jnp.bfloat16)
        values = values_ref[e]
        high = values.astype(jnp.bfloat16).astype(jnp.float32)
        low = values - high
        rows = [jnp.where(group == g, high, 0.0) for g in range(groups)]
        rows += [jnp.where(group == g, low, 0.0) for g in range(groups)]
        left = jnp.concatenate(rows, axis=0).astype(jnp.bfloat16)
        out = lax.dot_general(
            left, hot, (((1,), (1,)), ((), ())), preferred_element_type=jnp.float32
        )
        half = groups * proj
        total = out[:half] + out[half:]
        row = jnp.concatenate([total[g * proj : (g + 1) * proj] for g in range(groups)], axis=1)
        return row

    def pair(i, carry):
        both = jnp.concatenate([step(2 * i, None), step(2 * i + 1, None)], axis=0)
        high, low = split(both)
        at = pl.ds(pl.multiple_of(i * 2 * proj, 2 * proj), 2 * proj)
        dense_high[at, :] = high
        dense_low[at, :] = low
        return carry

    lax.fori_loop(0, tiles // 2, pair, 0)
    partials_ref[...] = dot3(
        (dense_high[...], dense_low[...]), (high_ref[...], low_ref[...])
    )


def project(tile_cells, projectors, field):
    entries, proj, tile = projectors.shape
    cell_count, bands = field.shape
    block = 16
    rows = block * proj
    flops = 2 * entries * (2 * proj * cell_count * tile + 3 * proj * cell_count * bands)
    return pl.pallas_call(
        project_kernel,
        grid=(entries // block,),
        in_specs=[
            pl.BlockSpec((block, tile), lambda i: (i, 0)),
            pl.BlockSpec((block, proj, tile), lambda i: (i, 0, 0)),
            pl.BlockSpec((cell_count, bands), lambda i: (0, 0)),
        ],
        out_specs=[
            pl.BlockSpec((rows, cell_count), lambda i: (i, 0)),
            pl.BlockSpec((rows, cell_count), lambda i: (i, 0)),
            pl.BlockSpec((rows, bands), lambda i: (i, 0)),
        ],
        out_shape=[
            jax.ShapeDtypeStruct((entries * proj, cell_count), jnp.bfloat16),
            jax.ShapeDtypeStruct((entries * proj, cell_count), jnp.bfloat16),
            jax.ShapeDtypeStruct((entries * proj, bands), jnp.float32),
        ],
        scratch_shapes=[pltpu.VMEM((cell_count, bands), jnp.bfloat16)] * 2,
        compiler_params=pltpu.CompilerParams(vmem_limit_bytes=32 * 2**20),
        cost_estimate=pl.CostEstimate(flops=8 * flops, bytes_accessed=2**24, transcendentals=0),
        name="project",
    )(tile_cells, projectors, field)


def exchange_kernel(
    sums_ref, coupling_ref, mats_ref, out_ref, arrived, mine, others,
    send_sums, recv_sums, send_mine, recv_mine, send_out, recv_out,
):
    dom_count, band_count = sums_ref.shape[0], mats_ref.shape[0]
    dom, band = lax.axis_index("dom"), lax.axis_index("band")
    mesh_id = pl.DeviceIdType.MESH
    barrier = pltpu.get_barrier_semaphore()

    def dom_peer(k):
        return lax.rem(dom + k, dom_count)

    def band_peer(k):
        return lax.rem(band + k, band_count)

    def greet(k, carry):
        pl.semaphore_signal(barrier, inc=1, device_id={"dom": dom_peer(k)}, device_id_type=mesh_id)
        return carry

    lax.fori_loop(1, dom_count, greet, 0)
    for k in range(1, band_count):
        pl.semaphore_signal(barrier, inc=1, device_id={"band": band_peer(k)}, device_id_type=mesh_id)
    pl.semaphore_wait(barrier, dom_count - 1 + band_count - 1)

    def sums_copy(k):
        return pltpu.make_async_remote_copy(
            src_ref=sums_ref.at[dom_peer(k)],
            dst_ref=arrived.at[k],
            send_sem=send_sums.at[k],
            recv_sem=recv_sums.at[k],
            device_id={"dom": dom_peer(k)},
            device_id_type=mesh_id,
        )

    def mine_copy(k):
        return pltpu.make_async_remote_copy(
            src_ref=mine,
            dst_ref=others.at[k],
            send_sem=send_mine.at[k],
            recv_sem=recv_mine.at[k],
            device_id={"band": band_peer(k)},
            device_id_type=mesh_id,
        )

    def out_copy(k):
        return pltpu.make_async_remote_copy(
            src_ref=out_ref.at[dom],
            dst_ref=out_ref.at[dom],
            send_sem=send_out.at[k],
            recv_sem=recv_out.at[k],
            device_id={"dom": dom_peer(k)},
            device_id_type=mesh_id,
        )

    def start(copy):
        def step(k, carry):
            copy(k).start()
            return carry

        return step

    def add(k, total):
        sums_copy(k).wait_recv()
        return total + arrived[k]

    lax.fori_loop(1, dom_count, start(sums_copy), 0)
    total = lax.fori_loop(1, dom_count, add, sums_ref[dom])
    mine[...] = dot3(split(coupling_ref[...]), split(total))
    for k in range(1, band_count):
        mine_copy(k).start()
    result = dot3(split(mine[...]), split(mats_ref[band]))
    for k in range(1, band_count):
        mine_copy(k).wait_recv()
        source = lax.rem(band - k + band_count, band_count)
        result = result + dot3(split(others[k]), split(mats_ref[source]))
    out_ref[dom] = result
    lax.fori_loop(1, dom_count, start(out_copy), 0)

    def finish(k, carry):
        source = lax.rem(dom - k + dom_count, dom_count)
        pltpu.make_async_remote_copy(
            src_ref=out_ref.at[dom],
            dst_ref=out_ref.at[source],
            send_sem=send_out.at[k],
            recv_sem=recv_out.at[k],
            device_id={"dom": dom_peer(k)},
            device_id_type=mesh_id,
        ).wait()
        sums_copy(k).wait_send()
        return carry

    lax.fori_loop(1, dom_count, finish, 0)
    for k in range(1, band_count):
        mine_copy(k).wait_send()


def exchange(sums, coupling, mats):
    dom_count, rows, bands = sums.shape
    band_count = mats.shape[0]
    vmem = pl.BlockSpec(memory_space=pltpu.VMEM)
    dma = pltpu.SemaphoreType.DMA
    return pl.pallas_call(
        exchange_kernel,
        in_specs=[vmem] * 3,
        out_specs=vmem,
        out_shape=jax.ShapeDtypeStruct(sums.shape, jnp.float32),
        scratch_shapes=[
            pltpu.VMEM(sums.shape, jnp.float32),
            pltpu.VMEM((rows, bands), jnp.float32),
            pltpu.VMEM((band_count, rows, bands), jnp.float32),
            dma((dom_count,)),
            dma((dom_count,)),
            dma((band_count,)),
            dma((band_count,)),
            dma((dom_count,)),
            dma((dom_count,)),
        ],
        compiler_params=pltpu.CompilerParams(
            vmem_limit_bytes=32 * 2**20, collective_id=0, has_side_effects=True
        ),
        cost_estimate=pl.CostEstimate(
            flops=6 * rows * band_count * bands * bands,
            bytes_accessed=2**24,
            transcendentals=0,
        ),
        name="exchange",
    )(sums, coupling, mats)


def spread_kernel(dense_high, dense_low, back_high, back_low, far_ref):
    dims = (((0,), (0,)), ((), ()))
    far_ref[...] = dot3(
        (dense_high[...], dense_low[...]), (back_high[...], back_low[...]), dims
    )


def spread(dense_high, dense_low, back):
    rows, cell_count = dense_high.shape
    bands = back.shape[1]
    block = 256
    back_high, back_low = split_outside(back)
    return pl.pallas_call(
        spread_kernel,
        grid=(cell_count // block,),
        in_specs=[
            pl.BlockSpec((rows, block), lambda i: (0, i)),
            pl.BlockSpec((rows, block), lambda i: (0, i)),
            pl.BlockSpec((rows, bands), lambda i: (0, 0)),
            pl.BlockSpec((rows, bands), lambda i: (0, 0)),
        ],
        out_specs=pl.BlockSpec((block, bands), lambda i: (i, 0)),
        out_shape=jax.ShapeDtypeStruct((cell_count, bands), jnp.float32),
        compiler_params=pltpu.CompilerParams(vmem_limit_bytes=32 * 2**20),
        cost_estimate=pl.CostEstimate(
            flops=6 * rows * cell_count * bands, bytes_accessed=2**24, transcendentals=0
        ),
        name="spread",
    )(dense_high, dense_low, back_high, back_low)


def rotate_kernel(count, *refs):
    blocks, mats, out_ref = refs[:count], refs[count:-1], refs[-1]
    total = None
    for block, mat in zip(blocks, mats):
        term = dot3(split(block[...]), split(mat[...]))
        total = term if total is None else total + term
    out_ref[...] = total


def rotate(blocks, mats):
    rows, depth = blocks[0].shape
    bands = mats[0].shape[1]
    block = 256
    return pl.pallas_call(
        functools.partial(rotate_kernel, len(blocks)),
        grid=(rows // block,),
        in_specs=[pl.BlockSpec((block, depth), lambda i: (i, 0))] * len(blocks)
        + [pl.BlockSpec((depth, bands), lambda i: (0, 0))] * len(mats),
        out_specs=pl.BlockSpec((block, bands), lambda i: (i, 0)),
        out_shape=jax.ShapeDtypeStruct((rows, bands), jnp.float32),
        compiler_params=pltpu.CompilerParams(vmem_limit_bytes=32 * 2**20),
        cost_estimate=pl.CostEstimate(
            flops=6 * rows * depth * len(blocks) * bands, bytes_accessed=2**22, transcendentals=0
        ),
        name="rotate",
    )(*blocks, *mats)


def local_kernel(count, sides, *refs):
    items, refs = refs[:count], refs[count:]
    before, refs = refs[:sides], refs[sides:]
    after, refs = refs[:sides], refs[sides:]
    weight_ref, far_ref, first_ref, second_ref = refs
    planes, ny = first_ref.shape[:2]
    step = ny // sides
    for i, item in enumerate(items):
        at = (i % sides) * step
        first_ref[i // sides, at : at + step] = item[...]
    for p in range(planes):
        here = first_ref[p]
        low = jnp.concatenate([r[...] for r in before], 0) if p == 0 else first_ref[p - 1]
        high = jnp.concatenate([r[...] for r in after], 0) if p == planes - 1 else first_ref[p + 1]
        beside = low + high
        beside = beside + jnp.roll(here, 1, 0) + jnp.roll(here, -1, 0)
        beside = beside + jnp.roll(here, 1, 1) + jnp.roll(here, -1, 1)
        second_ref[p] = weight_ref[p] * here - 0.5 * beside + far_ref[p]


def local_apply(items, before, after, weight, far):
    planes, ny, nz, bands = far.shape
    whole = pl.BlockSpec((planes, ny, nz, LANES), lambda i: (0, 0, 0, i))
    part = pl.BlockSpec((items[0].shape[0], nz, LANES), lambda i: (0, 0, i))
    return pl.pallas_call(
        functools.partial(local_kernel, len(items), len(before)),
        grid=(bands // LANES,),
        in_specs=[part] * (len(items) + 2 * len(before))
        + [pl.BlockSpec((planes, ny, nz, LANES), lambda i: (0, 0, 0, 0)), whole],
        out_specs=[whole, whole],
        out_shape=[jax.ShapeDtypeStruct(far.shape, jnp.float32)] * 2,
        compiler_params=pltpu.CompilerParams(vmem_limit_bytes=40 * 2**20),
        cost_estimate=pl.CostEstimate(
            flops=12 * planes * ny * nz * bands, bytes_accessed=2**23, transcendentals=0
        ),
        name="local",
    )(*items, *before, *after, weight, far)


def gather_blocks(field, parts):
    count = lax.axis_size("band")
    me = lax.axis_index("band")
    rows = field.shape[0] // parts
    pieces = [field[i * rows : (i + 1) * rows] for i in range(parts)]
    if count != 4:
        out = []
        for piece in pieces:
            whole = lax.all_gather(piece, "band", axis=0)
            out.append([whole[i] for i in range(count)])
        return out, list(range(count))
    flip = lambda k: [(i, i ^ k) for i in range(count)]
    direct = [
        (piece, lax.ppermute(piece, "band", flip(1)), lax.ppermute(piece, "band", flip(2)))
        for piece in pieces
    ]
    out = []
    for i, (piece, one, two) in enumerate(direct):
        three = lax.ppermute(one, "band", flip(2)) if i % 2 == 0 else lax.ppermute(two, "band", flip(1))
        out.append([piece, one, two, three])
    return out, [me ^ k for k in range(count)]


def body(orbitals, potential, projectors, tile_cells, tile_atom, atom_owner, coupling, rotation):
    planes, ny, nz, bands = orbitals.shape
    cell_count = planes * ny * nz
    entries, proj, _ = projectors.shape
    atom_total = atom_owner.shape[0]
    dom_count = lax.axis_size("dom")
    domain_index = lax.axis_index("dom")
    field = orbitals.reshape(cell_count, bands)
    sides = 2
    blocks, owners = gather_blocks(field, planes * sides)
    band_mats = rotation.reshape(-1, bands, bands)
    mats = [lax.dynamic_index_in_dim(band_mats, o, axis=0, keepdims=False) for o in owners]
    dense_high, dense_low, partials = project(tile_cells, projectors, field)
    my_atoms = lax.dynamic_slice_in_dim(tile_atom, domain_index * entries, entries)
    my_rows = owner_rows(my_atoms, atom_owner)
    columns = (my_rows[:, None] == jnp.arange(atom_total, dtype=jnp.int32)[None, :]).astype(
        jnp.float32
    )
    sums = jnp.einsum(
        "ea,ekb->akb",
        columns,
        partials.reshape(entries, proj, bands),
        precision=lax.Precision.HIGHEST,
    )
    own = coupling.shape[0]
    eye = jnp.eye(own, dtype=bool)[:, None, :, None]
    coupled = jnp.where(eye, coupling[:, :, None, :], 0.0).reshape(own * proj, own * proj)
    scaled = exchange(sums.reshape(dom_count, own * proj, bands), coupled, band_mats)
    scaled = scaled.reshape(atom_total, proj, bands)
    back = jnp.einsum("ea,akb->ekb", columns, scaled, precision=lax.Precision.HIGHEST)
    far = spread(dense_high, dense_low, back.reshape(entries * proj, bands))

    weight = jnp.broadcast_to((3.0 + potential)[..., None], (planes, ny, nz, LANES))
    rotated = [rotate(part, mats).reshape(-1, nz, bands) for part in blocks]
    down = [((i + 1) % dom_count, i) for i in range(dom_count)]
    up = [(i, (i + 1) % dom_count) for i in range(dom_count)]
    after = [lax.ppermute(item, "dom", down) for item in rotated[:sides]]
    before = [lax.ppermute(item, "dom", up) for item in rotated[-sides:]]
    first, second = local_apply(rotated, before, after, weight, far.reshape(orbitals.shape))
    return first, second


def solution(mesh):
    return jax.shard_map(
        body,
        mesh=mesh,
        in_specs=(
            P("dom", None, None, "band"),
            P("dom", None, None),
            P("dom", None, None),
            P("dom", None),
            P(),
            P(),
            P("dom", None, None),
            P(None, "band"),
        ),
        out_specs=(P("dom", None, None, "band"), P("dom", None, None, "band")),
        check_vma=False,
    )
```

```python
import functools

import jax
import jax.numpy as jnp
from jax import lax
from jax.experimental import pallas as pl
from jax.experimental.pallas import tpu as pltpu
from jax.sharding import PartitionSpec as P

LANES = 128
SUB = 8


def split(x):
    high = x.astype(jnp.bfloat16)
    low = (x - high.astype(jnp.float32)).astype(jnp.bfloat16)
    return high, low


def split_outside(x):
    high = lax.reduce_precision(x, exponent_bits=8, mantissa_bits=7)
    return high.astype(jnp.bfloat16), (x - high).astype(jnp.bfloat16)


def dot3(a, b, dims=(((1,), (0,)), ((), ()))):
    a_high, a_low = a
    b_high, b_low = b
    dot = functools.partial(lax.dot_general, dimension_numbers=dims, preferred_element_type=jnp.float32)
    return dot(a_high, b_high) + (dot(a_high, b_low) + dot(a_low, b_high))


def owner_rows(atom_ids, atom_owner):
    match = atom_ids[..., None] == jnp.arange(atom_owner.shape[0], dtype=jnp.int32)
    found_rows = jnp.sum(jnp.where(match, atom_owner, 0), axis=-1)
    return jnp.where(atom_ids >= 0, found_rows, -1)


def fused_kernel(
    cells_ref, values_ref, field_ref, keys_ref, coupling_ref, mats_ref,
    rot_ref, before_ref, after_ref, far_ref,
    dense_high, dense_low, field_high, field_low, partials, select, sums, arrived, mine, others,
    returned, one, two, three,
    send_one, recv_one, send_two, recv_two, send_three, recv_three,
    send_sums, recv_sums, send_mine, recv_mine, send_out, recv_out,
    send_before, recv_before, send_after, recv_after,
):
    entries, proj, tile = values_ref.shape
    groups = dense_high.shape[1] // LANES
    items, rows, bands = rot_ref.shape
    sides = before_ref.shape[0]
    dom_count, own, _ = sums.shape
    band_count = mats_ref.shape[0]
    dom, band = lax.axis_index("dom"), lax.axis_index("band")
    mesh_id = pl.DeviceIdType.MESH
    barrier = pltpu.get_barrier_semaphore()
    flip_one = band + 1 - 2 * lax.rem(band, 2)
    flip_two = lax.rem(band + 2, band_count)
    flip_three = lax.rem(flip_one + 2, band_count)

    def dom_peer(k):
        return lax.rem(dom + k, dom_count)

    def band_peer(k):
        return lax.rem(band + k, band_count)

    def remote(src, dst, send, recv, target):
        return pltpu.make_async_remote_copy(
            src_ref=src, dst_ref=dst, send_sem=send, recv_sem=recv,
            device_id=target, device_id_type=mesh_id,
        )

    def greet(k, carry):
        pl.semaphore_signal(barrier, inc=1, device_id={"dom": dom_peer(k)}, device_id_type=mesh_id)
        return carry

    lax.fori_loop(1, dom_count, greet, 0)
    for k in range(1, band_count):
        pl.semaphore_signal(barrier, inc=1, device_id={"band": band_peer(k)}, device_id_type=mesh_id)
    pl.semaphore_wait(barrier, dom_count - 1 + band_count - 1)

    def own_rows(i):
        return field_ref.at[pl.ds(i * rows, rows)]

    def one_copy(i):
        return remote(own_rows(i), one.at[i], send_one.at[i], recv_one.at[i], {"band": flip_one})

    def two_copy(i):
        return remote(own_rows(i), two.at[i], send_two.at[i], recv_two.at[i], {"band": flip_two})

    def three_copy(i):
        if i % 2 == 0:
            return remote(one.at[i], three.at[i], send_three.at[i], recv_three.at[i], {"band": flip_two})
        return remote(two.at[i], three.at[i], send_three.at[i], recv_three.at[i], {"band": flip_one})

    def forward(i):
        (one_copy if i % 2 == 0 else two_copy)(i).wait_recv()
        three_copy(i).start()

    for i in range(items):
        one_copy(i).start()
        two_copy(i).start()

    field_high[...], field_low[...] = split(field_ref[...])
    lane_ids = lax.broadcasted_iota(jnp.int32, (LANES, tile), 0)

    def dense_row(e):
        cells = cells_ref[pl.ds(e, 1), :]
        group = jnp.broadcast_to(cells // LANES, (proj, tile))
        spot = jnp.broadcast_to(cells % LANES, (LANES, tile))
        hot = jnp.where(spot == lane_ids, 1.0, 0.0).astype(jnp.bfloat16)
        values = values_ref[e]
        high = values.astype(jnp.bfloat16).astype(jnp.float32)
        low = values - high
        parts = [jnp.where(group == g, high, 0.0) for g in range(groups)]
        parts += [jnp.where(group == g, low, 0.0) for g in range(groups)]
        left = jnp.concatenate(parts, axis=0).astype(jnp.bfloat16)
        out = lax.dot_general(
            left, hot, (((1,), (1,)), ((), ())), preferred_element_type=jnp.float32
        )
        total = out[: groups * proj] + out[groups * proj :]
        return jnp.concatenate([total[g * proj : (g + 1) * proj] for g in range(groups)], axis=1)

    def pair(i, carry):
        both = jnp.concatenate([dense_row(2 * i), dense_row(2 * i + 1)], axis=0)
        at = pl.ds(pl.multiple_of(i * 2 * proj, 2 * proj), 2 * proj)
        dense_high[at, :], dense_low[at, :] = split(both)
        return carry

    block = 256

    def product(i, carry):
        at = pl.ds(pl.multiple_of(i * block, block), block)
        partials[at, :] = dot3(
            (dense_high[at, :], dense_low[at, :]), (field_high[...], field_low[...])
        )
        return carry

    pairs = entries // 2
    lax.fori_loop(0, pairs // 2, pair, 0)
    forward(0)
    lax.fori_loop(pairs // 2, pairs, pair, 0)
    lax.fori_loop(0, entries * proj // block, product, 0)
    forward(1)

    partial_high, partial_low = split(partials[...])

    def gather_sums(d, carry):
        ids = d * own + lax.broadcasted_iota(jnp.int32, (own, entries * proj), 0)
        hit = jnp.where(ids == keys_ref[...], 1.0, 0.0).astype(jnp.bfloat16)
        select[pl.ds(pl.multiple_of(d * own, own), own), :] = hit
        sums[d] = jnp.dot(hit, partial_high, preferred_element_type=jnp.float32) + jnp.dot(
            hit, partial_low, preferred_element_type=jnp.float32
        )
        return carry

    lax.fori_loop(0, dom_count, gather_sums, 0)

    def sums_copy(k):
        return remote(
            sums.at[dom_peer(k)], arrived.at[k], send_sums.at[k], recv_sums.at[k], {"dom": dom_peer(k)}
        )

    def mine_copy(k):
        return remote(mine, others.at[k], send_mine.at[k], recv_mine.at[k], {"band": band_peer(k)})

    def start_sums(k, carry):
        sums_copy(k).start()
        return carry

    def add(k, total):
        sums_copy(k).wait_recv()
        return total + arrived[k]

    lax.fori_loop(1, dom_count, start_sums, 0)
    total = lax.fori_loop(1, dom_count, add, sums[dom])
    mine[...] = dot3(split(coupling_ref[...]), split(total))
    for k in range(1, band_count):
        mine_copy(k).start()
    forward(2)
    result = dot3(split(mine[...]), split(mats_ref[band]))
    for k in range(1, band_count):
        mine_copy(k).wait_recv()
        source = lax.rem(band - k + band_count, band_count)
        result = result + dot3(split(others[k]), split(mats_ref[source]))
    returned[dom] = result

    def start_out(k, carry):
        remote(
            returned.at[dom], returned.at[dom], send_out.at[k], recv_out.at[k], {"dom": dom_peer(k)}
        ).start()
        return carry

    lax.fori_loop(1, dom_count, start_out, 0)
    for i in range(3, items):
        forward(i)

    def after_copy(i):
        return remote(
            rot_ref.at[i], after_ref.at[i], send_after.at[i], recv_after.at[i],
            {"dom": dom_peer(dom_count - 1)},
        )

    def before_copy(i):
        return remote(
            rot_ref.at[items - sides + i], before_ref.at[i], send_before.at[i], recv_before.at[i],
            {"dom": dom_peer(1)},
        )

    def rotate(i):
        (two_copy if i % 2 == 0 else one_copy)(i).wait_recv()
        three_copy(i).wait_recv()
        out = dot3(split(own_rows(i)[...]), split(mats_ref[band]))
        out = out + dot3(split(one[i]), split(mats_ref[flip_one]))
        out = out + dot3(split(two[i]), split(mats_ref[flip_two]))
        rot_ref[i] = out + dot3(split(three[i]), split(mats_ref[flip_three]))
        if i < sides:
            after_copy(i).start()
        if i >= items - sides:
            before_copy(i - (items - sides)).start()

    def finish_out(k, carry):
        source = lax.rem(dom - k + dom_count, dom_count)
        remote(
            returned.at[dom], returned.at[source], send_out.at[k], recv_out.at[k], {"dom": dom_peer(k)}
        ).wait()
        sums_copy(k).wait_send()
        return carry

    transposed = (((0,), (0,)), ((), ()))

    def far_sum():
        lax.fori_loop(1, dom_count, finish_out, 0)
        all_rows = returned[...].reshape(dom_count * own, bands)
        high, low = split(all_rows)
        back = lax.dot_general(
            select[...], high, transposed, preferred_element_type=jnp.float32
        ) + lax.dot_general(select[...], low, transposed, preferred_element_type=jnp.float32)
        back = split(back)
        for c in range(0, far_ref.shape[0], block):
            far_ref[c : c + block, :] = dot3(
                (dense_high[:, c : c + block], dense_low[:, c : c + block]), back, transposed
            )

    far_at = min(1, items - 1)
    for i in range(items):
        rotate(i)
        if i == far_at:
            far_sum()
    for i in range(sides):
        after_copy(i).wait()
        before_copy(i).wait()
    for i in range(items):
        one_copy(i).wait_send()
        two_copy(i).wait_send()
        three_copy(i).wait_send()
    for k in range(1, band_count):
        mine_copy(k).wait_send()


def fused(tile_cells, projectors, field, keys, coupling, mats, items, sides, dom_count):
    entries, proj, _ = projectors.shape
    cell_count, bands = field.shape
    band_count = mats.shape[0]
    own = coupling.shape[0]
    rows = cell_count // items
    vmem = pl.BlockSpec(memory_space=pltpu.VMEM)
    dma = pltpu.SemaphoreType.DMA
    f32, bf16 = jnp.float32, jnp.bfloat16
    return pl.pallas_call(
        fused_kernel,
        in_specs=[vmem] * 6,
        out_specs=[vmem] * 4,
        out_shape=[
            jax.ShapeDtypeStruct((items, rows, bands), f32),
            jax.ShapeDtypeStruct((sides, rows, bands), f32),
            jax.ShapeDtypeStruct((sides, rows, bands), f32),
            jax.ShapeDtypeStruct((cell_count, bands), f32),
        ],
        scratch_shapes=[
            pltpu.VMEM((entries * proj, cell_count), bf16),
            pltpu.VMEM((entries * proj, cell_count), bf16),
            pltpu.VMEM((cell_count, bands), bf16),
            pltpu.VMEM((cell_count, bands), bf16),
            pltpu.VMEM((entries * proj, bands), f32),
            pltpu.VMEM((dom_count * own, entries * proj), bf16),
            pltpu.VMEM((dom_count, own, bands), f32),
            pltpu.VMEM((dom_count, own, bands), f32),
            pltpu.VMEM((own, bands), f32),
            pltpu.VMEM((band_count, own, bands), f32),
            pltpu.VMEM((dom_count, own, bands), f32),
            pltpu.VMEM((items, rows, bands), f32),
            pltpu.VMEM((items, rows, bands), f32),
            pltpu.VMEM((items, rows, bands), f32),
        ]
        + [dma((items,))] * 6
        + [dma((dom_count,))] * 2
        + [dma((band_count,))] * 2
        + [dma((dom_count,))] * 2
        + [dma((sides,))] * 4,
        compiler_params=pltpu.CompilerParams(
            vmem_limit_bytes=60 * 2**20, collective_id=0, has_side_effects=True
        ),
        name="fused",
    )(tile_cells, projectors, field, keys, coupling, mats)


def local_kernel(field_ref, before_ref, after_ref, weight_ref, far_ref, first_ref, second_ref):
    planes = first_ref.shape[0]
    for p in range(planes):
        here = field_ref[p]
        first_ref[p] = here
        low = before_ref[...] if p == 0 else field_ref[p - 1]
        high = after_ref[...] if p == planes - 1 else field_ref[p + 1]
        beside = low + high
        beside = beside + jnp.roll(here, 1, 0) + jnp.roll(here, -1, 0)
        beside = beside + jnp.roll(here, 1, 1) + jnp.roll(here, -1, 1)
        second_ref[p] = weight_ref[p] * here - 0.5 * beside + far_ref[p]


def local_apply(field, before, after, weight, far):
    planes, ny, nz, bands = far.shape
    whole = pl.BlockSpec((planes, ny, nz, LANES), lambda i: (0, 0, 0, i))
    side = pl.BlockSpec((ny, nz, LANES), lambda i: (0, 0, i))
    return pl.pallas_call(
        local_kernel,
        grid=(bands // LANES,),
        in_specs=[whole, side, side]
        + [pl.BlockSpec((planes, ny, nz, LANES), lambda i: (0, 0, 0, 0)), whole],
        out_specs=[whole, whole],
        out_shape=[jax.ShapeDtypeStruct(far.shape, jnp.float32)] * 2,
        compiler_params=pltpu.CompilerParams(vmem_limit_bytes=40 * 2**20),
        name="local",
    )(field, before, after, weight, far)


def body(orbitals, potential, projectors, tile_cells, tile_atom, atom_owner, coupling, rotation):
    planes, ny, nz, bands = orbitals.shape
    cell_count = planes * ny * nz
    entries, proj, _ = projectors.shape
    atom_total = atom_owner.shape[0]
    dom_count = lax.axis_size("dom")
    domain_index = lax.axis_index("dom")
    field = orbitals.reshape(cell_count, bands)
    sides = 2
    band_mats = rotation.reshape(-1, bands, bands)
    my_atoms = lax.dynamic_slice_in_dim(tile_atom, domain_index * entries, entries)
    my_rows = owner_rows(my_atoms, atom_owner)
    keys = (my_rows[:, None] * proj + jnp.arange(proj, dtype=jnp.int32)).reshape(1, -1)
    own = coupling.shape[0]
    eye = jnp.eye(own, dtype=bool)[:, None, :, None]
    coupled = jnp.where(eye, coupling[:, :, None, :], 0.0).reshape(own * proj, own * proj)
    rotated, before, after, far = fused(
        tile_cells, projectors, field, keys, coupled, band_mats, planes * sides, sides, dom_count
    )
    weight = jnp.broadcast_to((3.0 + potential)[..., None], (planes, ny, nz, LANES))
    first, second = local_apply(
        rotated.reshape(orbitals.shape),
        before.reshape(ny, nz, bands),
        after.reshape(ny, nz, bands),
        weight,
        far.reshape(orbitals.shape),
    )
    return first, second


def solution(mesh):
    return jax.shard_map(
        body,
        mesh=mesh,
        in_specs=(
            P("dom", None, None, "band"),
            P("dom", None, None),
            P("dom", None, None),
            P("dom", None),
            P(),
            P(),
            P("dom", None, None),
            P(None, "band"),
        ),
        out_specs=(P("dom", None, None, "band"), P("dom", None, None, "band")),
        check_vma=False,
    )
```

```python
import functools

import jax
import jax.numpy as jnp
from jax import lax
from jax.experimental import pallas as pl
from jax.experimental.pallas import tpu as pltpu
from jax.sharding import PartitionSpec as P

LANES = 128
SUB = 8


def split(x):
    high = x.astype(jnp.bfloat16)
    low = (x - high.astype(jnp.float32)).astype(jnp.bfloat16)
    return high, low


def split_outside(x):
    high = lax.reduce_precision(x, exponent_bits=8, mantissa_bits=7)
    return high.astype(jnp.bfloat16), (x - high).astype(jnp.bfloat16)


def dot3(a, b, dims=(((1,), (0,)), ((), ()))):
    a_high, a_low = a
    b_high, b_low = b
    dot = functools.partial(lax.dot_general, dimension_numbers=dims, preferred_element_type=jnp.float32)
    return dot(a_high, b_high) + (dot(a_high, b_low) + dot(a_low, b_high))


def owner_rows(atom_ids, atom_owner):
    match = atom_ids[..., None] == jnp.arange(atom_owner.shape[0], dtype=jnp.int32)
    found_rows = jnp.sum(jnp.where(match, atom_owner, 0), axis=-1)
    return jnp.where(atom_ids >= 0, found_rows, -1)


def fused_kernel(
    cells_ref, values_ref, field_ref, keys_ref, coupling_ref, mats_ref,
    rot_ref, before_ref, after_ref, far_ref,
    dense_high, dense_low, field_high, field_low, partials, select, sums, arrived, mine, others,
    returned, one, two, three,
    send_one, recv_one, send_two, recv_two, send_three, recv_three,
    send_sums, recv_sums, send_mine, recv_mine, send_out, recv_out,
    send_before, recv_before, send_after, recv_after,
):
    entries, proj, tile = values_ref.shape
    groups = dense_high.shape[1] // LANES
    items, rows, bands = rot_ref.shape
    sides = before_ref.shape[0]
    dom_count, own, _ = sums.shape
    band_count = mats_ref.shape[0]
    dom, band = lax.axis_index("dom"), lax.axis_index("band")
    mesh_id = pl.DeviceIdType.MESH
    barrier = pltpu.get_barrier_semaphore()
    flip_one = band + 1 - 2 * lax.rem(band, 2)
    flip_two = lax.rem(band + 2, band_count)
    flip_three = lax.rem(flip_one + 2, band_count)

    def dom_peer(k):
        return lax.rem(dom + k, dom_count)

    def band_peer(k):
        return lax.rem(band + k, band_count)

    def remote(src, dst, send, recv, target):
        return pltpu.make_async_remote_copy(
            src_ref=src, dst_ref=dst, send_sem=send, recv_sem=recv,
            device_id=target, device_id_type=mesh_id,
        )

    def greet(k, carry):
        pl.semaphore_signal(barrier, inc=1, device_id={"dom": dom_peer(k)}, device_id_type=mesh_id)
        return carry

    lax.fori_loop(1, dom_count, greet, 0)
    for k in range(1, band_count):
        pl.semaphore_signal(barrier, inc=1, device_id={"band": band_peer(k)}, device_id_type=mesh_id)
    pl.semaphore_wait(barrier, dom_count - 1 + band_count - 1)

    def own_rows(i):
        return field_ref.at[pl.ds(i * rows, rows)]

    def one_copy(i):
        return remote(own_rows(i), one.at[i], send_one.at[i], recv_one.at[i], {"band": flip_one})

    def two_copy(i):
        return remote(own_rows(i), two.at[i], send_two.at[i], recv_two.at[i], {"band": flip_two})

    def three_copy(i):
        if i % 2 == 0:
            return remote(one.at[i], three.at[i], send_three.at[i], recv_three.at[i], {"band": flip_two})
        return remote(two.at[i], three.at[i], send_three.at[i], recv_three.at[i], {"band": flip_one})

    def forward(i):
        (one_copy if i % 2 == 0 else two_copy)(i).wait_recv()
        three_copy(i).start()

    for i in range(items):
        one_copy(i).start()
        two_copy(i).start()

    field_high[...], field_low[...] = split(field_ref[...])
    lane_ids = lax.broadcasted_iota(jnp.int32, (LANES, tile), 0)

    def dense_row(e):
        cells = cells_ref[pl.ds(e, 1), :]
        group = jnp.broadcast_to(cells // LANES, (proj, tile))
        spot = jnp.broadcast_to(cells % LANES, (LANES, tile))
        hot = jnp.where(spot == lane_ids, 1.0, 0.0).astype(jnp.bfloat16)
        values = values_ref[e]
        high = values.astype(jnp.bfloat16).astype(jnp.float32)
        low = values - high
        parts = [jnp.where(group == g, high, 0.0) for g in range(groups)]
        parts += [jnp.where(group == g, low, 0.0) for g in range(groups)]
        left = jnp.concatenate(parts, axis=0).astype(jnp.bfloat16)
        out = lax.dot_general(
            left, hot, (((1,), (1,)), ((), ())), preferred_element_type=jnp.float32
        )
        total = out[: groups * proj] + out[groups * proj :]
        return jnp.concatenate([total[g * proj : (g + 1) * proj] for g in range(groups)], axis=1)

    def pair(i, carry):
        both = jnp.concatenate([dense_row(2 * i), dense_row(2 * i + 1)], axis=0)
        at = pl.ds(pl.multiple_of(i * 2 * proj, 2 * proj), 2 * proj)
        dense_high[at, :], dense_low[at, :] = split(both)
        return carry

    block = 256

    def product(i, carry):
        at = pl.ds(pl.multiple_of(i * block, block), block)
        partials[at, :] = dot3(
            (dense_high[at, :], dense_low[at, :]), (field_high[...], field_low[...])
        )
        return carry

    pairs = entries // 2
    lax.fori_loop(0, pairs // 2, pair, 0)
    forward(0)
    lax.fori_loop(pairs // 2, pairs, pair, 0)
    lax.fori_loop(0, entries * proj // block, product, 0)
    forward(1)

    partial_high, partial_low = split(partials[...])

    def gather_sums(d, carry):
        ids = d * own + lax.broadcasted_iota(jnp.int32, (own, entries * proj), 0)
        hit = jnp.where(ids == keys_ref[...], 1.0, 0.0).astype(jnp.bfloat16)
        select[pl.ds(pl.multiple_of(d * own, own), own), :] = hit
        sums[d] = jnp.dot(hit, partial_high, preferred_element_type=jnp.float32) + jnp.dot(
            hit, partial_low, preferred_element_type=jnp.float32
        )
        return carry

    lax.fori_loop(0, dom_count, gather_sums, 0)

    def sums_copy(k):
        return remote(
            sums.at[dom_peer(k)], arrived.at[k], send_sums.at[k], recv_sums.at[k], {"dom": dom_peer(k)}
        )

    def mine_copy(k):
        return remote(mine, others.at[k], send_mine.at[k], recv_mine.at[k], {"band": band_peer(k)})

    def start_sums(k, carry):
        sums_copy(k).start()
        return carry

    def add(k, total):
        sums_copy(k).wait_recv()
        return total + arrived[k]

    lax.fori_loop(1, dom_count, start_sums, 0)
    for i in range(2, items):
        forward(i)
    total = lax.fori_loop(1, dom_count, add, sums[dom])
    mine[...] = dot3(split(coupling_ref[...]), split(total))
    for k in range(1, band_count):
        mine_copy(k).start()

    def start_out(k, carry):
        remote(
            returned.at[dom], returned.at[dom], send_out.at[k], recv_out.at[k], {"dom": dom_peer(k)}
        ).start()
        return carry

    def return_sums():
        result = dot3(split(mine[...]), split(mats_ref[band]))
        for k in range(1, band_count):
            mine_copy(k).wait_recv()
            source = lax.rem(band - k + band_count, band_count)
            result = result + dot3(split(others[k]), split(mats_ref[source]))
        returned[dom] = result
        lax.fori_loop(1, dom_count, start_out, 0)

    def after_copy(i):
        return remote(
            rot_ref.at[i], after_ref.at[i], send_after.at[i], recv_after.at[i],
            {"dom": dom_peer(dom_count - 1)},
        )

    def before_copy(i):
        return remote(
            rot_ref.at[items - sides + i], before_ref.at[i], send_before.at[i], recv_before.at[i],
            {"dom": dom_peer(1)},
        )

    def rotate(i):
        (two_copy if i % 2 == 0 else one_copy)(i).wait_recv()
        three_copy(i).wait_recv()
        out = dot3(split(own_rows(i)[...]), split(mats_ref[band]))
        out = out + dot3(split(one[i]), split(mats_ref[flip_one]))
        out = out + dot3(split(two[i]), split(mats_ref[flip_two]))
        rot_ref[i] = out + dot3(split(three[i]), split(mats_ref[flip_three]))
        if i < sides:
            after_copy(i).start()
        if i >= items - sides:
            before_copy(i - (items - sides)).start()

    def finish_out(k, carry):
        source = lax.rem(dom - k + dom_count, dom_count)
        remote(
            returned.at[dom], returned.at[source], send_out.at[k], recv_out.at[k], {"dom": dom_peer(k)}
        ).wait()
        sums_copy(k).wait_send()
        return carry

    transposed = (((0,), (0,)), ((), ()))

    def far_sum():
        lax.fori_loop(1, dom_count, finish_out, 0)
        all_rows = returned[...].reshape(dom_count * own, bands)
        high, low = split(all_rows)
        back = lax.dot_general(
            select[...], high, transposed, preferred_element_type=jnp.float32
        ) + lax.dot_general(select[...], low, transposed, preferred_element_type=jnp.float32)
        back = split(back)
        for c in range(0, far_ref.shape[0], block):
            far_ref[c : c + block, :] = dot3(
                (dense_high[:, c : c + block], dense_low[:, c : c + block]), back, transposed
            )

    rotate(0)
    return_sums()
    for i in range(1, items):
        rotate(i)
    far_sum()
    for i in range(sides):
        after_copy(i).wait()
        before_copy(i).wait()
    for i in range(items):
        one_copy(i).wait_send()
        two_copy(i).wait_send()
        three_copy(i).wait_send()
    for k in range(1, band_count):
        mine_copy(k).wait_send()


def fused(tile_cells, projectors, field, keys, coupling, mats, items, sides, dom_count):
    entries, proj, _ = projectors.shape
    cell_count, bands = field.shape
    band_count = mats.shape[0]
    own = coupling.shape[0]
    rows = cell_count // items
    vmem = pl.BlockSpec(memory_space=pltpu.VMEM)
    dma = pltpu.SemaphoreType.DMA
    f32, bf16 = jnp.float32, jnp.bfloat16
    dense_bytes = 4 * entries * proj * (cell_count + bands)
    sums_bytes = 12 * dom_count * own * bands + 2 * dom_count * own * entries * proj
    scratch_bytes = dense_bytes + sums_bytes + 16 * cell_count * bands
    return pl.pallas_call(
        fused_kernel,
        in_specs=[vmem] * 6,
        out_specs=[vmem] * 4,
        out_shape=[
            jax.ShapeDtypeStruct((items, rows, bands), f32),
            jax.ShapeDtypeStruct((sides, rows, bands), f32),
            jax.ShapeDtypeStruct((sides, rows, bands), f32),
            jax.ShapeDtypeStruct((cell_count, bands), f32),
        ],
        scratch_shapes=[
            pltpu.VMEM((entries * proj, cell_count), bf16),
            pltpu.VMEM((entries * proj, cell_count), bf16),
            pltpu.VMEM((cell_count, bands), bf16),
            pltpu.VMEM((cell_count, bands), bf16),
            pltpu.VMEM((entries * proj, bands), f32),
            pltpu.VMEM((dom_count * own, entries * proj), bf16),
            pltpu.VMEM((dom_count, own, bands), f32),
            pltpu.VMEM((dom_count, own, bands), f32),
            pltpu.VMEM((own, bands), f32),
            pltpu.VMEM((band_count, own, bands), f32),
            pltpu.VMEM((dom_count, own, bands), f32),
            pltpu.VMEM((items, rows, bands), f32),
            pltpu.VMEM((items, rows, bands), f32),
            pltpu.VMEM((items, rows, bands), f32),
        ]
        + [dma((items,))] * 6
        + [dma((dom_count,))] * 2
        + [dma((band_count,))] * 2
        + [dma((dom_count,))] * 2
        + [dma((sides,))] * 4,
        compiler_params=pltpu.CompilerParams(
            vmem_limit_bytes=min(60 * 2**20, scratch_bytes + sums_bytes // 2 + 12 * 2**20), collective_id=0, has_side_effects=True
        ),
        name="fused",
    )(tile_cells, projectors, field, keys, coupling, mats)


def local_kernel(field_ref, before_ref, after_ref, weight_ref, far_ref, first_ref, second_ref):
    planes = first_ref.shape[0]
    for p in range(planes):
        here = field_ref[p]
        first_ref[p] = here
        low = before_ref[...] if p == 0 else field_ref[p - 1]
        high = after_ref[...] if p == planes - 1 else field_ref[p + 1]
        beside = low + high
        beside = beside + jnp.roll(here, 1, 0) + jnp.roll(here, -1, 0)
        beside = beside + jnp.roll(here, 1, 1) + jnp.roll(here, -1, 1)
        second_ref[p] = weight_ref[p] * here - 0.5 * beside + far_ref[p]


def local_apply(field, before, after, weight, far):
    planes, ny, nz, bands = far.shape
    whole = pl.BlockSpec((planes, ny, nz, LANES), lambda i: (0, 0, 0, i))
    side = pl.BlockSpec((ny, nz, LANES), lambda i: (0, 0, i))
    return pl.pallas_call(
        local_kernel,
        grid=(bands // LANES,),
        in_specs=[whole, side, side]
        + [pl.BlockSpec((planes, ny, nz, LANES), lambda i: (0, 0, 0, 0)), whole],
        out_specs=[whole, whole],
        out_shape=[jax.ShapeDtypeStruct(far.shape, jnp.float32)] * 2,
        compiler_params=pltpu.CompilerParams(vmem_limit_bytes=20 * 2**20),
        name="local",
    )(field, before, after, weight, far)


def body(orbitals, potential, projectors, tile_cells, tile_atom, atom_owner, coupling, rotation):
    planes, ny, nz, bands = orbitals.shape
    cell_count = planes * ny * nz
    entries, proj, _ = projectors.shape
    atom_total = atom_owner.shape[0]
    dom_count = lax.axis_size("dom")
    domain_index = lax.axis_index("dom")
    field = orbitals.reshape(cell_count, bands)
    sides = 2
    band_mats = rotation.reshape(-1, bands, bands)
    my_atoms = lax.dynamic_slice_in_dim(tile_atom, domain_index * entries, entries)
    my_rows = owner_rows(my_atoms, atom_owner)
    keys = (my_rows[:, None] * proj + jnp.arange(proj, dtype=jnp.int32)).reshape(1, -1)
    own = coupling.shape[0]
    eye = jnp.eye(own, dtype=bool)[:, None, :, None]
    coupled = jnp.where(eye, coupling[:, :, None, :], 0.0).reshape(own * proj, own * proj)
    rotated, before, after, far = fused(
        tile_cells, projectors, field, keys, coupled, band_mats, planes * sides, sides, dom_count
    )
    weight = jnp.broadcast_to((3.0 + potential)[..., None], (planes, ny, nz, LANES))
    first, second = local_apply(
        rotated.reshape(orbitals.shape),
        before.reshape(ny, nz, bands),
        after.reshape(ny, nz, bands),
        weight,
        far.reshape(orbitals.shape),
    )
    return first, second


def solution(mesh):
    return jax.shard_map(
        body,
        mesh=mesh,
        in_specs=(
            P("dom", None, None, "band"),
            P("dom", None, None),
            P("dom", None, None),
            P("dom", None),
            P(),
            P(),
            P("dom", None, None),
            P(None, "band"),
        ),
        out_specs=(P("dom", None, None, "band"), P("dom", None, None, "band")),
        check_vma=False,
    )
```
